512 devices in a mesh: row: 16 (over x, z_lo), col: 32 (over z_hi, y, core).
Axes of the slice: x: 4, y: 4, z: 16 (z_hi: 4, z_lo: 4; z = z_hi * 4 + z_lo), core: 2. Of those that a mesh axis runs over, the one named last changes fastest.
Arguments:
- spectra: bfloat16 [2048, 2, 128, 128], P(('row', 'col')), may hold values from -3600 to 3600
- kept_windows: int32 [128], replicated, may hold values 0 or 1
Outputs:
- correlations: float32 [2048, 32, 64, 128], P('row', 'col')
The draws below stay inside these ranges and needn't reach their ends.
All inputs are finite; a program needn't handle non-finite values.
Results may differ from the reference program's by a relative error of at most 0.0025.
Values may be sent and summed in bfloat16 or wider, within the bound.
A program may use at most 128 MiB of HBM per device.

```python
import math
import jax
import jax.numpy as jnp
from jax import lax

NF = 128
WIN = 128
CPD = 4
CHANNELS = 2048
FIRST_BLK = 128
SECOND_BLK = 64
N_ROW = 16
N_COL = 32


def draw_spectra(key, part):
    keys = jax.random.split(key, 3)
    positions = jnp.arange(CHANNELS, dtype=jnp.float32) / max(CHANNELS - 1, 1)
    ramp = jnp.exp(math.log(3.0) * positions)
    noise = jnp.clip(jax.random.normal(keys[0], (CHANNELS, 2, NF, WIN), jnp.float32), -4.0, 4.0)
    rough = jnp.exp(jax.random.uniform(keys[1], (CHANNELS,), jnp.float32, 0.0, math.log(10.0)))
    loudness = jnp.exp(jax.random.uniform(keys[2], (WIN,), jnp.float32, 0.0, math.log(10.0)))
    return (noise * (ramp * rough)[:, None, None, None] * loudness[None, None, None, :]).astype(jnp.bfloat16)


def with_ends(drawn, stream_key, low, largest):
    dims = drawn.shape
    place = [jax.random.randint(jax.random.fold_in(stream_key, axis), (), 0, dims[axis]) for axis in range(len(dims))]
    drawn = drawn.at[tuple(place)].set(low)
    longest = dims.index(max(dims))
    place[longest] = (place[longest] + 1) % dims[longest]
    return drawn.at[tuple(place)].set(largest)


def setup_inputs(seed: int = 0) -> dict:
    arg_keys = jax.random.split(jax.random.key(seed), 3)
    spectra = draw_spectra(jax.random.fold_in(arg_keys[2], 71), 0)
    kept_windows = with_ends((jax.random.randint(arg_keys[1], (WIN,), 0, 4) < 3).astype(jnp.int32), jax.random.fold_in(arg_keys[1], 1), 0, 1)
    return dict(spectra=spectra, kept_windows=kept_windows)


EPSILON = 1e-06

def reference(spectra, kept_windows):
    spec_float = spectra.astype(jnp.float32)
    energy = lax.optimization_barrier(jnp.sum(spec_float * spec_float, axis=(0, 1, 2))) / (CHANNELS * 2 * NF) + EPSILON
    factor = kept_windows.astype(jnp.float32) / energy
    weighted = (spec_float * factor).astype(jnp.bfloat16)
    weighted = lax.optimization_barrier(weighted).astype(jnp.float32)
    partners = spec_float.reshape(N_ROW, N_COL, CPD, 2, NF, WIN)
    partners = partners.transpose(1, 0, 2, 3, 4, 5).reshape(N_COL, SECOND_BLK, 2, NF, WIN)
    first_blocks = weighted.reshape(N_ROW, FIRST_BLK, 2, NF, WIN)
    highest = lax.Precision.HIGHEST

    def block_lags(first_rows):
        real_a = first_rows[:, 0]
        imag_a = first_rows[:, 1]
        real_b = partners[:, :, 0]
        imag_b = partners[:, :, 1]
        real_s = jnp.einsum('afw,cbfw->acbf', real_a, real_b, precision=highest)
        real_s = real_s + jnp.einsum('afw,cbfw->acbf', imag_a, imag_b, precision=highest)
        imag_s = jnp.einsum('afw,cbfw->acbf', imag_a, real_b, precision=highest)
        imag_s = imag_s - jnp.einsum('afw,cbfw->acbf', real_a, imag_b, precision=highest)
        spectrum = lax.complex(real_s, imag_s)
        return jnp.real(jnp.fft.ifft(spectrum, axis=-1)) * (NF / math.sqrt(NF * WIN))
    lag_blocks = lax.map(block_lags, first_blocks)
    return lag_blocks.reshape(CHANNELS, N_COL, SECOND_BLK, NF).astype(jnp.float32)
```

```python
import functools
import math

import jax
import jax.numpy as jnp
import numpy as np
from jax import lax
from jax.experimental import pallas as pl
from jax.experimental.pallas import tpu as pltpu
from jax.sharding import PartitionSpec as P

EPSILON = 1e-06
MESH = pl.DeviceIdType.MESH
WAVES = 2
CHUNK = 16
WAVE = 2 * CHUNK
REACH = ((8, 4), (4, 8))
ORDER = [(0, 1), (1, 0)]
for _s in range(2, 9):
    ORDER += [(0, _s), (1, _s - 1)]
ORDER += [(1, 8)]


def gather_stack(spectra, kept, stack, zbuf, abuf, bbuf, tmp, ebuf, factor,
                 zs, zr, xs, xr, xs2, xr2, ys, yr, ys2, yr2, cs, cr, la, lb, es, er):
    row = lax.axis_index("row")
    col = lax.axis_index("col")
    x, zl = row // 4, row % 4
    zh, y, core = col // 8, (col // 2) % 4, col % 2
    z = zh * 4 + zl

    def at(dx=0, dy=0, dz=0, dzl=0, dzh=0, dc=0):
        new_z = (z + dz + 16) % 16
        new_zl = (new_z % 4 + dzl) % 4
        new_zh = (new_z // 4 + dzh) % 4
        return (
            (x + dx + 4) % 4 * 4 + new_zl,
            new_zh * 8 + (y + dy + 4) % 4 * 2 + (core + dc) % 2,
        )

    peers = [at(dz=1), at(dz=-1), at(dc=1)]
    for p in (1, 2, 3):
        peers += [at(dx=p), at(dy=p), at(dzl=p), at(dzh=p)]
    barrier = pltpu.get_barrier_semaphore()
    for peer in peers:
        pl.semaphore_signal(barrier, inc=1, device_id=peer, device_id_type=MESH)

    channels = spectra.shape[0]
    total = jnp.zeros((8, 128), jnp.float32)
    for part in range(2):
        for t in range(channels):
            plane = spectra[t, part].astype(jnp.float32)
            total = total + jnp.sum((plane * plane).reshape(16, 8, 128), axis=0)
            tmp[pl.ds(part * channels + t, 128, stride=8), :] = plane
    zbuf[z] = tmp[...].reshape(64, 16, 128).astype(jnp.bfloat16)
    pl.semaphore_wait(barrier, len(peers))

    def remote(src, dst, send, recv, device):
        return pltpu.make_async_remote_copy(
            src_ref=src, dst_ref=dst, send_sem=send, recv_sem=recv, device_id=device, device_id_type=MESH
        )

    rounds = [("dx", x, 4), ("dy", y, 4), ("dzl", zl, 4), ("dzh", zh, 4), ("dc", core, 2)]

    def energy_copies(k):
        name, place, size = rounds[k]
        return [
            remote(ebuf.at[k, place], ebuf.at[k, place], es.at[k, p], er.at[k, p], at(**{name: p}))
            for p in range(1, size)
        ]

    def energy_start(k, value):
        ebuf[k, rounds[k][1]] = value
        for copy in energy_copies(k):
            copy.start()

    def energy_finish(k):
        for copy in energy_copies(k):
            copy.wait()
        return jnp.sum(ebuf[k, : rounds[k][2]], axis=0)

    def z_copy(side, s, w, h):
        slot = (z - s + 16) % 16 if side == 0 else (z + s) % 16
        part = zbuf.at[slot, pl.ds(w * WAVE + h * CHUNK, CHUNK)]
        return remote(part, part, zs.at[side, s, w, h], zr.at[side, s, w, h], at(dz=1 if side == 0 else -1))

    def z_arrived(side, s, w, h):
        slot = (z - s + 16) % 16 if side == 0 else (z + s) % 16
        part = zbuf.at[slot, pl.ds(w * WAVE + h * CHUNK, CHUNK)]
        remote(part, part, zs.at[side, s - 1, w, h], zr.at[side, s - 1, w, h], at(dz=1)).wait_recv()

    def wave(w):
        return pl.ds(w * WAVE, WAVE)

    def half(w, h):
        return pl.ds(w * WAVE + h * CHUNK, CHUNK)

    def x_first(side, unit, w):
        return remote(
            zbuf.at[zh * 4 + unit, wave(w)], bbuf.at[x * 4 + unit, wave(w)],
            xs.at[side, unit, w], xr.at[side, unit, w], at(dx=1 if side == 0 else -1),
        )

    def x_source(side, unit):
        return (x + (3 if side == 0 else 1)) % 4 * 4 + unit

    def x_arrived(side, unit, w):
        part = bbuf.at[x_source(side, unit), wave(w)]
        remote(part, part, xs.at[side, unit, w], xr.at[side, unit, w], at(dx=1)).wait_recv()

    def x_second(side, unit, w):
        part = bbuf.at[x_source(side, unit), half(w, side)]
        return remote(part, part, xs2.at[side, unit, w], xr2.at[side, unit, w], at(dx=1 if side == 0 else -1))

    def x_second_arrived(side, unit, w):
        part = bbuf.at[(x + 2) % 4 * 4 + unit, half(w, side)]
        remote(part, part, xs2.at[side, unit, w], xr2.at[side, unit, w], at(dx=1)).wait_recv()

    def z_high(unit):
        return (zh + (0, 3, 1, 2)[unit]) % 4

    def y_first(side, unit, w):
        return remote(
            zbuf.at[z_high(unit) * 4 + zl, wave(w)], abuf.at[z_high(unit) * 4 + y, core, wave(w)],
            ys.at[side, unit, w], yr.at[side, unit, w], at(dy=1 if side == 0 else -1),
        )

    def y_slot(unit, dy):
        return z_high(unit) * 4 + (y + dy + 4) % 4

    def y_arrived(side, unit, w):
        part = abuf.at[y_slot(unit, -1 if side == 0 else 1), core, wave(w)]
        remote(part, part, ys.at[side, unit, w], yr.at[side, unit, w], at(dy=1)).wait_recv()

    def y_second(side, unit, w):
        part = abuf.at[y_slot(unit, -1 if side == 0 else 1), core, half(w, side)]
        return remote(part, part, ys2.at[side, unit, w], yr2.at[side, unit, w], at(dy=1 if side == 0 else -1))

    def y_second_arrived(side, unit, w):
        part = abuf.at[y_slot(unit, 2), core, half(w, side)]
        remote(part, part, ys2.at[side, unit, w], yr2.at[side, unit, w], at(dy=1)).wait_recv()

    def core_copy(which, unit, w):
        slot = y_slot(unit, (0, -1, 1, 2)[which])
        src = zbuf.at[z_high(unit) * 4 + zl, wave(w)] if which == 0 else abuf.at[slot, core, wave(w)]
        return remote(src, abuf.at[slot, core, wave(w)], cs.at[which, unit, w], cr.at[which, unit, w], at(dc=1))

    def core_arrived(which, unit, w):
        slot = y_slot(unit, (0, -1, 1, 2)[which])
        part = abuf.at[slot, 1 - core, wave(w)]
        remote(part, part, cs.at[which, unit, w], cr.at[which, unit, w], at(dc=1)).wait_recv()

    def own_a(unit, w):
        return pltpu.make_async_copy(
            zbuf.at[z_high(unit) * 4 + zl, wave(w)], abuf.at[y_slot(unit, 0), core, wave(w)], la.at[unit, w]
        )

    def own_b(w):
        return pltpu.make_async_copy(
            zbuf.at[pl.ds(zh * 4, 4), wave(w)], bbuf.at[pl.ds(x * 4, 4), wave(w)], lb.at[w]
        )

    def y_send(unit, w):
        y_first(0, unit, w).start()
        y_first(1, unit, w).start()
        core_copy(0, unit, w).start()
        own_a(unit, w).start()

    def y_pass(unit, w):
        for side in range(2):
            y_arrived(side, unit, w)
            y_second(side, unit, w).start()
            core_copy(1 + side, unit, w).start()

    def y_end(unit, w):
        y_second_arrived(0, unit, w)
        y_second_arrived(1, unit, w)
        core_copy(3, unit, w).start()

    def x_send(unit, w):
        x_first(0, unit, w).start()
        x_first(1, unit, w).start()

    def x_pass(unit, w):
        for side in range(2):
            x_arrived(side, unit, w)
            x_second(side, unit, w).start()

    def in_block(s, act):
        if s == 0:
            act(zl)
        elif s < 4:
            pl.when(zl >= s)(lambda: act(zl - s))
            pl.when(zl + s < 4)(lambda: act(zl + s))

    def z_step(w, s):
        if s == 0:
            for side in range(2):
                for h in ((0, 1) if side == 0 else (1, 0)):
                    z_copy(side, 0, w, h).start()
        else:
            for h in range(2):
                for side in ((0, 1) if h == 0 else (1, 0)):
                    if s <= REACH[h][side]:
                        z_arrived(side, s, w, h)
                        if s < REACH[h][side]:
                            z_copy(side, s, w, h).start()
        if s == 0:
            y_send(0, w)
        if s == 4:
            y_send(1, w)
            y_send(2, w)
        if s == 8:
            y_send(3, w)
        in_block(s, lambda unit: x_send(unit, w))
        if s == 3:
            own_b(w).start()
        if s >= 2:
            in_block(s - 2, lambda unit: x_pass(unit, w))
        if s == 2:
            y_pass(0, w)
        if s == 4:
            y_end(0, w)
        if s == 6:
            y_pass(1, w)
            y_pass(2, w)
        if s == 8:
            y_end(1, w)
            y_end(2, w)

    energy_start(0, total)
    z_step(0, 0)
    stage = 0
    for w, s in ORDER:
        z_step(w, s)
        if w == 0 and stage < 5:
            value = energy_finish(stage)
            stage += 1
            if stage < 5:
                energy_start(stage, value)
            else:
                members = channels * lax.axis_size("row") * lax.axis_size("col")
                energy = jnp.sum(value, axis=0, keepdims=True) / (members * 2 * 128) + EPSILON
                factor[...] = kept[...].astype(jnp.float32) / energy

    def finish(w):
        y_pass(3, w)
        y_end(3, w)
        for unit in range(4):
            for side in range(2):
                x_second_arrived(side, unit, w)
        own_b(w).wait()
        for unit in range(4):
            own_a(unit, w).wait()
        for which in range(4):
            for unit in range(4):
                core_arrived(which, unit, w)

    low_rows = lax.broadcasted_iota(jnp.int32, (1, 8, 128), 1) < 4

    def split_parts(both):
        even, odd = both[:, 0], both[:, 1]
        real = jnp.where(low_rows, even, pltpu.roll(odd, 4, 1))
        imag = jnp.where(low_rows, pltpu.roll(even, 4, 1), odd)
        return real, imag

    def stack_pair(pair, carry):
        first = abuf[:, :, pair].astype(jnp.float32)
        second = bbuf[:, pair].astype(jnp.float32).reshape(8, 2, 16, 128)
        weight = factor[...].reshape(1, 1, 128)
        for odd in range(2):
            real, imag = split_parts(first[:, :, odd * 8 : odd * 8 + 8])
            left = jnp.concatenate(
                [(real * weight).reshape(128, 128), (imag * weight).reshape(128, 128)], axis=1
            ).astype(jnp.bfloat16)
            real, imag = split_parts(second[:, :, odd * 8 : odd * 8 + 8])
            real, imag = real.reshape(64, 128), imag.reshape(64, 128)
            right = jnp.concatenate(
                [jnp.concatenate([real, imag], axis=1), jnp.concatenate([-imag, real], axis=1)], axis=0
            ).astype(jnp.bfloat16)
            stack[2 * pair + odd] = lax.dot_general(
                left, right, (((1,), (1,)), ((), ())), preferred_element_type=jnp.float32
            )
        return carry

    for w in range(WAVES):
        finish(w)
        lax.fori_loop(w * WAVE, (w + 1) * WAVE, stack_pair, 0)

    for w in range(WAVES):
        for side in range(2):
            for h in range(2):
                for s in range(REACH[h][side]):
                    z_copy(side, s, w, h).wait_send()
            for unit in range(4):
                x_first(side, unit, w).wait_send()
                x_second(side, unit, w).wait_send()
                y_first(side, unit, w).wait_send()
                y_second(side, unit, w).wait_send()
        for which in range(4):
            for unit in range(4):
                core_copy(which, unit, w).wait_send()


A_BLK = 8


def lag_kernel(stack, high, low, out):
    first = pl.program_id(0) * A_BLK
    rows = []
    for i in range(A_BLK):
        bins = stack[:, pl.ds(first + i, 1), :].reshape(128, 128).astype(jnp.bfloat16)
        flipped = bins.T
        rows.append(jnp.concatenate([flipped[:64], flipped[64:]], axis=1))
    left = jnp.concatenate(rows, axis=0)
    lags = jnp.dot(left, high[...], preferred_element_type=jnp.float32)
    lags = lags + jnp.dot(left, low[...], preferred_element_type=jnp.float32)
    out[...] = lags.reshape(A_BLK, 1, 64, 128)


def lag_tables():
    bins = np.arange(128)
    phases = (bins[:, None] * bins[None, :] % 128) * (2.0 * math.pi / 128)
    table = np.concatenate([np.cos(phases), -np.sin(phases)], axis=0) / math.sqrt(128 * 128)
    high = table.astype(jnp.bfloat16)
    low = (table - high.astype(np.float64)).astype(jnp.bfloat16)
    return high, low


def body(spectra, kept_windows):
    dma = pltpu.SemaphoreType.DMA
    vmem = pl.BlockSpec(memory_space=pltpu.VMEM)
    stack = pl.pallas_call(
        gather_stack,
        out_shape=jax.ShapeDtypeStruct((128, 128, 128), jnp.float32),
        in_specs=[vmem, vmem],
        out_specs=vmem,
        scratch_shapes=[
            pltpu.VMEM((16, 64, 16, 128), jnp.bfloat16),
            pltpu.VMEM((16, 2, 64, 16, 128), jnp.bfloat16),
            pltpu.VMEM((16, 64, 16, 128), jnp.bfloat16),
            pltpu.VMEM((1024, 128), jnp.float32),
            pltpu.VMEM((5, 4, 8, 128), jnp.float32),
            pltpu.VMEM((1, 128), jnp.float32),
            dma((2, 8, 2, 2)), dma((2, 8, 2, 2)),
            dma((2, 4, 2)), dma((2, 4, 2)), dma((2, 4, 2)), dma((2, 4, 2)),
            dma((2, 4, 2)), dma((2, 4, 2)), dma((2, 4, 2)), dma((2, 4, 2)),
            dma((4, 4, 2)), dma((4, 4, 2)),
            dma((4, 2)), dma((2,)),
            dma((5, 4)), dma((5, 4)),
        ],
        compiler_params=pltpu.CompilerParams(
            collective_id=0, has_side_effects=True, vmem_limit_bytes=40 << 20
        ),
        name="gather_stack",
    )(spectra, kept_windows.reshape(1, 128))
    high, low = lag_tables()
    return pl.pallas_call(
        lag_kernel,
        grid=(128 // A_BLK,),
        out_shape=jax.ShapeDtypeStruct((128, 1, 64, 128), jnp.float32),
        in_specs=[vmem, vmem, vmem],
        out_specs=pl.BlockSpec((A_BLK, 1, 64, 128), lambda i: (i, 0, 0, 0)),
        compiler_params=pltpu.CompilerParams(vmem_limit_bytes=40 << 20),
        name="lags",
    )(stack, jnp.asarray(high), jnp.asarray(low))


def solution(mesh):
    placed = (P(("row", "col"), None, None, None), P())
    return jax.shard_map(
        body, mesh=mesh, in_specs=placed, out_specs=P("row", "col", None, None), check_vma=False
    )
```

```python
import functools
import math

import jax
import jax.numpy as jnp
import numpy as np
from jax import lax
from jax.experimental import pallas as pl
from jax.experimental.pallas import tpu as pltpu
from jax.sharding import PartitionSpec as P

EPSILON = 1e-06
MESH = pl.DeviceIdType.MESH
WAVES = 2
CHUNK = 16
WAVE = 2 * CHUNK
REACH = ((8, 4), (4, 8))
ORDER = [(1, 0)] + [(_w, _s) for _s in range(1, 9) for _w in range(WAVES)]
TILES = 64
STEP = 8


def gather_stack(spectra_hbm, kept_hbm, stack, zbuf, abuf, bbuf, rhs, spectra, kept, tmp, ebuf, factor,
                 zs, zr, xs, xr, xs2, xr2, ys, yr, ys2, yr2, cs, cr, la, lb, es, er, ls):
    row = lax.axis_index("row")
    col = lax.axis_index("col")
    x, zl = row // 4, row % 4
    zh, y, core = col // 8, (col // 2) % 4, col % 2
    z = zh * 4 + zl

    def at(dx=0, dy=0, dz=0, dzl=0, dzh=0, dc=0):
        new_z = (z + dz + 16) % 16
        new_zl = (new_z % 4 + dzl) % 4
        new_zh = (new_z // 4 + dzh) % 4
        return (
            (x + dx + 4) % 4 * 4 + new_zl,
            new_zh * 8 + (y + dy + 4) % 4 * 2 + (core + dc) % 2,
        )

    peers = [at(dz=1), at(dz=-1), at(dc=1)]
    for p in (1, 2, 3):
        peers += [at(dx=p), at(dy=p), at(dzl=p), at(dzh=p)]
    barrier = pltpu.get_barrier_semaphore()
    for peer in peers:
        pl.semaphore_signal(barrier, inc=1, device_id=peer, device_id_type=MESH)

    loads = [pltpu.make_async_copy(spectra_hbm, spectra, ls.at[0]), pltpu.make_async_copy(kept_hbm, kept, ls.at[1])]
    for load in loads:
        load.start()
    for load in loads:
        load.wait()

    channels = spectra.shape[0]
    to = lax.broadcasted_iota(jnp.int32, (TILES, TILES), 0)
    source = lax.broadcasted_iota(jnp.int32, (TILES, TILES), 1)
    mirror = ((to + source == TILES) | (to + source == 0)).astype(jnp.float32).astype(jnp.bfloat16)
    total = jnp.zeros((8, 128), jnp.float32)
    for part in range(2):
        for t in range(channels):
            plane = spectra[t, part].astype(jnp.float32)
            total = total + jnp.sum((plane * plane).reshape(16, 8, 128), axis=0)
            mirrored = jnp.dot(mirror, spectra[t, part, TILES:], preferred_element_type=jnp.float32)
            tmp[pl.ds(part * channels + t, TILES, stride=16), :] = plane[:TILES]
            tmp[pl.ds(8 + part * channels + t, TILES, stride=16), :] = mirrored
    zbuf[z] = tmp[...].reshape(TILES, 16, 128).astype(jnp.bfloat16)
    pl.semaphore_wait(barrier, len(peers))

    def remote(src, dst, send, recv, device):
        return pltpu.make_async_remote_copy(
            src_ref=src, dst_ref=dst, send_sem=send, recv_sem=recv, device_id=device, device_id_type=MESH
        )

    rounds = [("dx", x, 4), ("dy", y, 4), ("dzl", zl, 4), ("dzh", zh, 4), ("dc", core, 2)]

    def energy_copies(k):
        name, place, size = rounds[k]
        return [
            remote(ebuf.at[k, place], ebuf.at[k, place], es.at[k, p], er.at[k, p], at(**{name: p}))
            for p in range(1, size)
        ]

    def energy_start(k, value):
        ebuf[k, rounds[k][1]] = value
        for copy in energy_copies(k):
            copy.start()

    def energy_finish(k):
        for copy in energy_copies(k):
            copy.wait()
        return jnp.sum(ebuf[k, : rounds[k][2]], axis=0)

    def z_copy(side, s, w, h):
        slot = (z - s + 16) % 16 if side == 0 else (z + s) % 16
        part = zbuf.at[slot, pl.ds(w * WAVE + h * CHUNK, CHUNK)]
        return remote(part, part, zs.at[side, s, w, h], zr.at[side, s, w, h], at(dz=1 if side == 0 else -1))

    def z_arrived(side, s, w, h):
        slot = (z - s + 16) % 16 if side == 0 else (z + s) % 16
        part = zbuf.at[slot, pl.ds(w * WAVE + h * CHUNK, CHUNK)]
        remote(part, part, zs.at[side, s - 1, w, h], zr.at[side, s - 1, w, h], at(dz=1)).wait_recv()

    def wave(w):
        return pl.ds(w * WAVE, WAVE)

    def half(w, h):
        return pl.ds(w * WAVE + h * CHUNK, CHUNK)

    def x_first(side, unit, w):
        return remote(
            zbuf.at[zh * 4 + unit, wave(w)], bbuf.at[x * 4 + unit, wave(w)],
            xs.at[side, unit, w], xr.at[side, unit, w], at(dx=1 if side == 0 else -1),
        )

    def x_source(side, unit):
        return (x + (3 if side == 0 else 1)) % 4 * 4 + unit

    def x_arrived(side, unit, w):
        part = bbuf.at[x_source(side, unit), wave(w)]
        remote(part, part, xs.at[side, unit, w], xr.at[side, unit, w], at(dx=1)).wait_recv()

    def x_second(side, unit, w):
        part = bbuf.at[x_source(side, unit), half(w, side)]
        return remote(part, part, xs2.at[side, unit, w], xr2.at[side, unit, w], at(dx=1 if side == 0 else -1))

    def x_second_arrived(side, unit, w):
        part = bbuf.at[(x + 2) % 4 * 4 + unit, half(w, side)]
        remote(part, part, xs2.at[side, unit, w], xr2.at[side, unit, w], at(dx=1)).wait_recv()

    def z_high(unit):
        return (zh + (0, 3, 1, 2)[unit]) % 4

    def y_first(side, unit, w):
        return remote(
            zbuf.at[z_high(unit) * 4 + zl, wave(w)], abuf.at[z_high(unit) * 4 + y, core, wave(w)],
            ys.at[side, unit, w], yr.at[side, unit, w], at(dy=1 if side == 0 else -1),
        )

    def y_slot(unit, dy):
        return z_high(unit) * 4 + (y + dy + 4) % 4

    def y_arrived(side, unit, w):
        part = abuf.at[y_slot(unit, -1 if side == 0 else 1), core, wave(w)]
        remote(part, part, ys.at[side, unit, w], yr.at[side, unit, w], at(dy=1)).wait_recv()

    def y_second(side, unit, w):
        part = abuf.at[y_slot(unit, -1 if side == 0 else 1), core, half(w, side)]
        return remote(part, part, ys2.at[side, unit, w], yr2.at[side, unit, w], at(dy=1 if side == 0 else -1))

    def y_second_arrived(side, unit, w):
        part = abuf.at[y_slot(unit, 2), core, half(w, side)]
        remote(part, part, ys2.at[side, unit, w], yr2.at[side, unit, w], at(dy=1)).wait_recv()

    def core_copy(which, unit, w):
        slot = y_slot(unit, (0, -1, 1, 2)[which])
        src = zbuf.at[z_high(unit) * 4 + zl, wave(w)] if which == 0 else abuf.at[slot, core, wave(w)]
        return remote(src, abuf.at[slot, core, wave(w)], cs.at[which, unit, w], cr.at[which, unit, w], at(dc=1))

    def core_arrived(which, unit, w):
        slot = y_slot(unit, (0, -1, 1, 2)[which])
        part = abuf.at[slot, 1 - core, wave(w)]
        remote(part, part, cs.at[which, unit, w], cr.at[which, unit, w], at(dc=1)).wait_recv()

    def own_a(unit, w):
        return pltpu.make_async_copy(
            zbuf.at[z_high(unit) * 4 + zl, wave(w)], abuf.at[y_slot(unit, 0), core, wave(w)], la.at[unit, w]
        )

    def own_b(w):
        return pltpu.make_async_copy(
            zbuf.at[pl.ds(zh * 4, 4), wave(w)], bbuf.at[pl.ds(x * 4, 4), wave(w)], lb.at[w]
        )

    def y_send(unit, w):
        y_first(0, unit, w).start()
        y_first(1, unit, w).start()
        core_copy(0, unit, w).start()
        own_a(unit, w).start()

    def y_pass(unit, w):
        for side in range(2):
            y_arrived(side, unit, w)
            y_second(side, unit, w).start()
            core_copy(1 + side, unit, w).start()

    def y_end(unit, w):
        y_second_arrived(0, unit, w)
        y_second_arrived(1, unit, w)
        core_copy(3, unit, w).start()

    def x_send(unit, w):
        x_first(0, unit, w).start()
        x_first(1, unit, w).start()

    def x_pass(unit, w):
        for side in range(2):
            x_arrived(side, unit, w)
            x_second(side, unit, w).start()

    def in_block(s, act):
        if s == 0:
            act(zl)
        elif s < 4:
            pl.when(zl >= s)(lambda: act(zl - s))
            pl.when(zl + s < 4)(lambda: act(zl + s))

    def z_step(w, s):
        if s == 0:
            for side in range(2):
                for h in ((0, 1) if side == 0 else (1, 0)):
                    z_copy(side, 0, w, h).start()
        else:
            for h in range(2):
                for side in ((0, 1) if h == 0 else (1, 0)):
                    if s <= REACH[h][side]:
                        z_arrived(side, s, w, h)
                        if s < REACH[h][side]:
                            z_copy(side, s, w, h).start()
        if s == 0:
            y_send(0, w)
        if s == 4:
            y_send(1, w)
            y_send(2, w)
        if s == 8:
            y_send(3, w)
        in_block(s, lambda unit: x_send(unit, w))
        if s == 3:
            own_b(w).start()
        if s >= 2:
            in_block(s - 2, lambda unit: x_pass(unit, w))
        if s == 2:
            y_pass(0, w)
        if s == 4:
            y_end(0, w)
        if s == 6:
            y_pass(1, w)
            y_pass(2, w)
        if s == 8:
            y_end(1, w)
            y_end(2, w)

    energy_start(0, total)
    z_step(0, 0)
    stage = 0
    for w, s in ORDER:
        z_step(w, s)
        if w == 0 and stage < 5:
            value = energy_finish(stage)
            stage += 1
            if stage < 5:
                energy_start(stage, value)
            else:
                members = channels * lax.axis_size("row") * lax.axis_size("col")
                energy = jnp.sum(value, axis=0, keepdims=True) / (members * 2 * 128) + EPSILON
                factor[...] = kept[...].astype(jnp.float32) / energy

    def finish_b(w):
        for unit in range(4):
            for side in range(2):
                x_second_arrived(side, unit, w)
        own_b(w).wait()

    def finish_a(unit, w):
        own_a(unit, w).wait()
        for which in range(4):
            core_arrived(which, unit, w)

    low_rows = lax.broadcasted_iota(jnp.int32, (1, 8, 128), 1) < 4

    def split_parts(both):
        even, odd = both[:, 0], both[:, 1]
        real = jnp.where(low_rows, even, pltpu.roll(odd, 4, 1))
        imag = jnp.where(low_rows, pltpu.roll(even, 4, 1), odd)
        return real.reshape(-1, 128), imag.reshape(-1, 128)

    def over_tiles(w, act):
        def step(i, carry):
            for k in range(STEP):
                act(w * WAVE + i * STEP + k)
            return carry

        lax.fori_loop(0, WAVE // STEP, step, 0)

    def make_rhs(tile):
        second = bbuf[:, tile].astype(jnp.float32).reshape(8, 2, 16, 128)
        real, imag = split_parts(second[:, :, :8])
        real_m, imag_m = split_parts(second[:, :, 8:])
        ends = tile == 0
        keep = jnp.where(ends, 0.0, 1.0)
        upper = jnp.concatenate([real, imag, real_m * keep, imag_m * keep], axis=1)
        lower = jnp.concatenate(
            [-imag * keep, real * keep, jnp.where(ends, real_m, imag_m), jnp.where(ends, imag_m, -real_m)], axis=1
        )
        rhs[tile] = jnp.concatenate([upper, lower], axis=0).astype(jnp.bfloat16)

    def make_stack(units):
        def act(tile):
            weight = factor[...]
            rows = []
            for unit in units:
                first = abuf[pl.ds(z_high(unit) * 4, 4), :, tile].astype(jnp.float32)
                parts = split_parts(first[:, :, :8]) + split_parts(first[:, :, 8:])
                rows.append(jnp.concatenate([part * weight for part in parts], axis=1).astype(jnp.bfloat16))
            sums = lax.dot_general(
                jnp.concatenate(rows, axis=0), rhs[tile], (((1,), (1,)), ((), ())), preferred_element_type=jnp.float32
            )
            for i, unit in enumerate(units):
                stack[pl.ds(z_high(unit) * (32 * TILES) + tile, 32, stride=TILES), :] = sums[32 * i : 32 * i + 32]

        return act

    for w in range(WAVES):
        finish_b(w)
        over_tiles(w, make_rhs)
        y_pass(3, w)
    for w in range(WAVES):
        finish_a(0, w)
        over_tiles(w, make_stack([0]))
    for w in range(WAVES):
        y_end(3, w)
        finish_a(1, w)
        finish_a(2, w)
        over_tiles(w, make_stack([1, 2]))
    for w in range(WAVES):
        finish_a(3, w)
        over_tiles(w, make_stack([3]))

    for w in range(WAVES):
        for side in range(2):
            for h in range(2):
                for s in range(REACH[h][side]):
                    z_copy(side, s, w, h).wait_send()
            for unit in range(4):
                x_first(side, unit, w).wait_send()
                x_second(side, unit, w).wait_send()
                y_first(side, unit, w).wait_send()
                y_second(side, unit, w).wait_send()
        for which in range(4):
            for unit in range(4):
                core_copy(which, unit, w).wait_send()


A_BLK = 32


def lag_kernel(stack, high, low, out):
    first = pl.program_id(0) * A_BLK
    rows = []
    for i in range(0, A_BLK, 2):
        start = pl.multiple_of((first + i) * TILES, 2 * TILES)
        flipped = stack[pl.ds(start, 2 * TILES), :].astype(jnp.bfloat16).T
        rows.append(jnp.concatenate([flipped[:64], flipped[64:]], axis=1))
    left = jnp.concatenate(rows, axis=0)
    lags = jnp.dot(left, high[...], preferred_element_type=jnp.float32)
    lags = lags + jnp.dot(left, low[...], preferred_element_type=jnp.float32)
    for i in range(0, A_BLK, 2):
        out[i, 0] = lags[32 * i : 32 * i + 64, :128]
        out[i + 1, 0] = lags[32 * i : 32 * i + 64, 128:]


def lag_tables():
    bins = np.arange(TILES)[:, None]
    lags = np.arange(128)[None, :]
    phases = (bins * lags % 128) * (2.0 * math.pi / 128)
    sines = -np.sin(phases)
    sines[0] = np.cos(math.pi * np.arange(128))
    table = np.zeros((2, 2, TILES, 2, 128))
    for i in range(2):
        table[0, i, :, i] = np.cos(phases)
        table[1, i, :, i] = sines
    table = table.reshape(4 * TILES, 256) / math.sqrt(128 * 128)
    high = table.astype(jnp.bfloat16)
    low = (table - high.astype(np.float64)).astype(jnp.bfloat16)
    return high, low


def body(spectra, kept_windows):
    dma = pltpu.SemaphoreType.DMA
    vmem = pl.BlockSpec(memory_space=pltpu.VMEM)
    stack = pl.pallas_call(
        gather_stack,
        out_shape=jax.ShapeDtypeStruct((128 * TILES, 128), jnp.float32),
        in_specs=[pl.BlockSpec(memory_space=pl.ANY)] * 2,
        out_specs=vmem,
        scratch_shapes=[
            pltpu.VMEM((16, 64, 16, 128), jnp.bfloat16),
            pltpu.VMEM((16, 2, 64, 16, 128), jnp.bfloat16),
            pltpu.VMEM((16, 64, 16, 128), jnp.bfloat16),
            pltpu.VMEM((TILES, 128, 512), jnp.bfloat16),
            pltpu.VMEM(spectra.shape, spectra.dtype),
            pltpu.VMEM((1, 128), jnp.int32),
            pltpu.VMEM((1024, 128), jnp.float32),
            pltpu.VMEM((5, 4, 8, 128), jnp.float32),
            pltpu.VMEM((1, 128), jnp.float32),
            dma((2, 8, 2, 2)), dma((2, 8, 2, 2)),
            dma((2, 4, 2)), dma((2, 4, 2)), dma((2, 4, 2)), dma((2, 4, 2)),
            dma((2, 4, 2)), dma((2, 4, 2)), dma((2, 4, 2)), dma((2, 4, 2)),
            dma((4, 4, 2)), dma((4, 4, 2)),
            dma((4, 2)), dma((2,)),
            dma((5, 4)), dma((5, 4)), dma((2,)),
        ],
        compiler_params=pltpu.CompilerParams(
            collective_id=0, has_side_effects=True, vmem_limit_bytes=40 << 20
        ),
        name="gather_stack",
    )(spectra, kept_windows.reshape(1, 128))
    high, low = lag_tables()
    return pl.pallas_call(
        lag_kernel,
        grid=(128 // A_BLK,),
        out_shape=jax.ShapeDtypeStruct((128, 1, 64, 128), jnp.float32),
        in_specs=[vmem, vmem, vmem],
        out_specs=pl.BlockSpec((A_BLK, 1, 64, 128), lambda i: (i, 0, 0, 0)),
        compiler_params=pltpu.CompilerParams(vmem_limit_bytes=40 << 20),
        name="lags",
    )(stack, jnp.asarray(high), jnp.asarray(low))


def solution(mesh):
    placed = (P(("row", "col"), None, None, None), P())
    return jax.shard_map(
        body, mesh=mesh, in_specs=placed, out_specs=P("row", "col", None, None), check_vma=False
    )
```

```python
import functools
import math

import jax
import jax.numpy as jnp
import numpy as np
from jax import lax
from jax.experimental import pallas as pl
from jax.experimental.pallas import tpu as pltpu
from jax.sharding import PartitionSpec as P

EPSILON = 1e-06
MESH = pl.DeviceIdType.MESH
WAVES = 2
CHUNK = 16
WAVE = 2 * CHUNK
BLOCK = 4
ORDER = [(1, 0)] + [(_w, _s) for _s in range(1, 5) for _w in range(WAVES)]
TILES = 64
STEP = 8


def gather_stack(spectra_hbm, kept_hbm, stack, zbuf, abuf, bbuf, rhs, spectra, kept, tmp, ebuf, factor,
                 zs, zr, xs, xr, xs2, xr2, ys, yr, ys2, yr2, cs, cr, la, lb, es, er, ls):
    row = lax.axis_index("row")
    col = lax.axis_index("col")
    x, zl = row // 4, row % 4
    zh, y, core = col // 8, (col // 2) % 4, col % 2
    z = zh * 4 + zl

    def at(dx=0, dy=0, dz=0, dzl=0, dzh=0, dc=0):
        new_z = (z + dz + 16) % 16
        new_zl = (new_z % 4 + dzl) % 4
        new_zh = (new_z // 4 + dzh) % 4
        return (
            (x + dx + 4) % 4 * 4 + new_zl,
            new_zh * 8 + (y + dy + 4) % 4 * 2 + (core + dc) % 2,
        )

    peers = [at(dz=1), at(dz=-1), at(dc=1)]
    for p in (1, 2, 3):
        peers += [at(dx=p), at(dy=p), at(dzl=p), at(dzh=p)]
    barrier = pltpu.get_barrier_semaphore()
    for peer in peers:
        pl.semaphore_signal(barrier, inc=1, device_id=peer, device_id_type=MESH)

    loads = [pltpu.make_async_copy(spectra_hbm, spectra, ls.at[0]), pltpu.make_async_copy(kept_hbm, kept, ls.at[1])]
    for load in loads:
        load.start()
    for load in loads:
        load.wait()

    channels = spectra.shape[0]
    to = lax.broadcasted_iota(jnp.int32, (TILES, TILES), 0)
    source = lax.broadcasted_iota(jnp.int32, (TILES, TILES), 1)
    mirror = ((to + source == TILES) | (to + source == 0)).astype(jnp.float32).astype(jnp.bfloat16)
    total = jnp.zeros((8, 128), jnp.float32)
    for part in range(2):
        for t in range(channels):
            plane = spectra[t, part].astype(jnp.float32)
            total = total + jnp.sum((plane * plane).reshape(16, 8, 128), axis=0)
            mirrored = jnp.dot(mirror, spectra[t, part, TILES:], preferred_element_type=jnp.float32)
            tmp[pl.ds(part * channels + t, TILES, stride=16), :] = plane[:TILES]
            tmp[pl.ds(8 + part * channels + t, TILES, stride=16), :] = mirrored
    zbuf[z] = tmp[...].reshape(TILES, 16, 128).astype(jnp.bfloat16)
    pl.semaphore_wait(barrier, len(peers))

    def remote(src, dst, send, recv, device):
        return pltpu.make_async_remote_copy(
            src_ref=src, dst_ref=dst, send_sem=send, recv_sem=recv, device_id=device, device_id_type=MESH
        )

    rounds = [("dx", x, 4), ("dy", y, 4), ("dzl", zl, 4), ("dzh", zh, 4), ("dc", core, 2)]

    def energy_copies(k):
        name, place, size = rounds[k]
        return [
            remote(ebuf.at[k, place], ebuf.at[k, place], es.at[k, p], er.at[k, p], at(**{name: p}))
            for p in range(1, size)
        ]

    def energy_start(k, value):
        ebuf[k, rounds[k][1]] = value
        for copy in energy_copies(k):
            copy.start()

    def energy_finish(k):
        for copy in energy_copies(k):
            copy.wait()
        return jnp.sum(ebuf[k, : rounds[k][2]], axis=0)

    def z_part(side, s, w, h):
        slot = (z - s + 16) % 16 if side == 0 else (z + s) % 16
        return zbuf.at[slot, pl.ds(w * WAVE + h * CHUNK, CHUNK)]

    def z_copy(side, s, w, h):
        part = z_part(side, s, w, h)
        hops = (1 if s < BLOCK else BLOCK) * (1 if side == 0 else -1)
        return remote(part, part, zs.at[side, s, w, h], zr.at[side, s, w, h], at(dz=hops))

    def z_arrived(side, s, w, h):
        part = z_part(side, s, w, h)
        sent = min(s - 1, BLOCK)
        remote(part, part, zs.at[side, sent, w, h], zr.at[side, sent, w, h], at(dz=1)).wait_recv()

    def wave(w):
        return pl.ds(w * WAVE, WAVE)

    def half(w, h):
        return pl.ds(w * WAVE + h * CHUNK, CHUNK)

    def x_first(side, unit, w):
        return remote(
            zbuf.at[zh * 4 + unit, wave(w)], bbuf.at[x * 4 + unit, wave(w)],
            xs.at[side, unit, w], xr.at[side, unit, w], at(dx=1 if side == 0 else -1),
        )

    def x_source(side, unit):
        return (x + (3 if side == 0 else 1)) % 4 * 4 + unit

    def x_arrived(side, unit, w):
        part = bbuf.at[x_source(side, unit), wave(w)]
        remote(part, part, xs.at[side, unit, w], xr.at[side, unit, w], at(dx=1)).wait_recv()

    def x_second(side, unit, w):
        part = bbuf.at[x_source(side, unit), half(w, side)]
        return remote(part, part, xs2.at[side, unit, w], xr2.at[side, unit, w], at(dx=1 if side == 0 else -1))

    def x_second_arrived(side, unit, w):
        part = bbuf.at[(x + 2) % 4 * 4 + unit, half(w, side)]
        remote(part, part, xs2.at[side, unit, w], xr2.at[side, unit, w], at(dx=1)).wait_recv()

    def z_high(unit):
        return (zh + (0, 3, 1, 2)[unit]) % 4

    def y_first(side, unit, w):
        return remote(
            zbuf.at[z_high(unit) * 4 + zl, wave(w)], abuf.at[z_high(unit) * 4 + y, core, wave(w)],
            ys.at[side, unit, w], yr.at[side, unit, w], at(dy=1 if side == 0 else -1),
        )

    def y_slot(unit, dy):
        return z_high(unit) * 4 + (y + dy + 4) % 4

    def y_arrived(side, unit, w):
        part = abuf.at[y_slot(unit, -1 if side == 0 else 1), core, wave(w)]
        remote(part, part, ys.at[side, unit, w], yr.at[side, unit, w], at(dy=1)).wait_recv()

    def y_second(side, unit, w):
        part = abuf.at[y_slot(unit, -1 if side == 0 else 1), core, half(w, side)]
        return remote(part, part, ys2.at[side, unit, w], yr2.at[side, unit, w], at(dy=1 if side == 0 else -1))

    def y_second_arrived(side, unit, w):
        part = abuf.at[y_slot(unit, 2), core, half(w, side)]
        remote(part, part, ys2.at[side, unit, w], yr2.at[side, unit, w], at(dy=1)).wait_recv()

    def core_copy(which, unit, w):
        slot = y_slot(unit, (0, -1, 1, 2)[which])
        src = zbuf.at[z_high(unit) * 4 + zl, wave(w)] if which == 0 else abuf.at[slot, core, wave(w)]
        return remote(src, abuf.at[slot, core, wave(w)], cs.at[which, unit, w], cr.at[which, unit, w], at(dc=1))

    def core_arrived(which, unit, w):
        slot = y_slot(unit, (0, -1, 1, 2)[which])
        part = abuf.at[slot, 1 - core, wave(w)]
        remote(part, part, cs.at[which, unit, w], cr.at[which, unit, w], at(dc=1)).wait_recv()

    def own_a(unit, w):
        return pltpu.make_async_copy(
            zbuf.at[z_high(unit) * 4 + zl, wave(w)], abuf.at[y_slot(unit, 0), core, wave(w)], la.at[unit, w]
        )

    def own_b(w):
        return pltpu.make_async_copy(
            zbuf.at[pl.ds(zh * 4, 4), wave(w)], bbuf.at[pl.ds(x * 4, 4), wave(w)], lb.at[w]
        )

    def y_send(unit, w):
        y_first(0, unit, w).start()
        y_first(1, unit, w).start()
        core_copy(0, unit, w).start()
        own_a(unit, w).start()

    def y_pass(unit, w):
        for side in range(2):
            y_arrived(side, unit, w)
            y_second(side, unit, w).start()
            core_copy(1 + side, unit, w).start()

    def y_end(unit, w):
        y_second_arrived(0, unit, w)
        y_second_arrived(1, unit, w)
        core_copy(3, unit, w).start()

    def x_send(unit, w):
        x_first(0, unit, w).start()
        x_first(1, unit, w).start()

    def x_pass(unit, w):
        for side in range(2):
            x_arrived(side, unit, w)
            x_second(side, unit, w).start()

    def in_block(s, act):
        if s == 0:
            act(zl)
        elif s < 4:
            pl.when(zl >= s)(lambda: act(zl - s))
            pl.when(zl + s < 4)(lambda: act(zl + s))

    def z_step(w, s):
        for h in range(2):
            for side in (h, 1 - h):
                if s > 0:
                    z_arrived(side, s, w, h)
                if s < BLOCK or side == h:
                    z_copy(side, s, w, h).start()
        if s == 0:
            y_send(0, w)
        if s == BLOCK:
            y_send(1, w)
            y_send(2, w)
        in_block(s, lambda unit: x_send(unit, w))
        if s == 3:
            own_b(w).start()
        if s >= 2:
            in_block(s - 2, lambda unit: x_pass(unit, w))
        if s == 2:
            y_pass(0, w)
        if s == 4:
            y_end(0, w)

    def z_last(w):
        for side in range(2):
            z_arrived(side, 2 * BLOCK, w, side)
        y_send(3, w)

    energy_start(0, total)
    z_step(0, 0)
    stage = 0
    for w, s in ORDER:
        z_step(w, s)
        if w == 0:
            energy_start(stage + 1, energy_finish(stage))
            stage += 1

    def finish_b(w):
        for unit in range(4):
            for side in range(2):
                x_second_arrived(side, unit, w)
        own_b(w).wait()

    def finish_a(unit, w):
        own_a(unit, w).wait()
        for which in range(4):
            core_arrived(which, unit, w)

    low_rows = lax.broadcasted_iota(jnp.int32, (1, 8, 128), 1) < 4

    def split_parts(both):
        even, odd = both[:, 0], both[:, 1]
        real = jnp.where(low_rows, even, pltpu.roll(odd, 4, 1))
        imag = jnp.where(low_rows, pltpu.roll(even, 4, 1), odd)
        return real.reshape(-1, 128), imag.reshape(-1, 128)

    def over_tiles(w, act):
        def step(i, carry):
            for k in range(STEP):
                act(w * WAVE + i * STEP + k)
            return carry

        lax.fori_loop(0, WAVE // STEP, step, 0)

    def make_rhs(tile):
        second = bbuf[:, tile].astype(jnp.float32).reshape(8, 2, 16, 128)
        real, imag = split_parts(second[:, :, :8])
        real_m, imag_m = split_parts(second[:, :, 8:])
        ends = tile == 0
        keep = jnp.where(ends, 0.0, 1.0)
        upper = jnp.concatenate([real, imag, real_m * keep, imag_m * keep], axis=1)
        lower = jnp.concatenate(
            [-imag * keep, real * keep, jnp.where(ends, real_m, imag_m), jnp.where(ends, imag_m, -real_m)], axis=1
        )
        rhs[tile] = jnp.concatenate([upper, lower], axis=0).astype(jnp.bfloat16)

    def make_stack(units):
        def act(tile):
            weight = factor[...]
            rows = []
            for unit in units:
                first = abuf[pl.ds(z_high(unit) * 4, 4), :, tile].astype(jnp.float32)
                parts = split_parts(first[:, :, :8]) + split_parts(first[:, :, 8:])
                rows.append(jnp.concatenate([part * weight for part in parts], axis=1).astype(jnp.bfloat16))
            sums = lax.dot_general(
                jnp.concatenate(rows, axis=0), rhs[tile], (((1,), (1,)), ((), ())), preferred_element_type=jnp.float32
            )
            for i, unit in enumerate(units):
                stack[pl.ds(z_high(unit) * (32 * TILES) + tile, 32, stride=TILES), :] = sums[32 * i : 32 * i + 32]

        return act

    for w in range(WAVES):
        y_pass(1, w)
        y_pass(2, w)
        in_block(3, lambda unit: x_pass(unit, w))
    value = energy_finish(4)
    members = channels * lax.axis_size("row") * lax.axis_size("col")
    energy = jnp.sum(value, axis=0, keepdims=True) / (members * 2 * 128) + EPSILON
    factor[...] = kept[...].astype(jnp.float32) / energy
    for w in range(WAVES):
        finish_b(w)
        over_tiles(w, make_rhs)
        y_end(1, w)
        y_end(2, w)
        z_last(w)
    y_pass(3, 0)
    for w in range(WAVES):
        finish_a(0, w)
        finish_a(1, w)
        finish_a(2, w)
        over_tiles(w, make_stack([0, 1, 2]))
        if w == 0:
            y_pass(3, 1)
            y_end(3, 0)
    y_end(3, 1)
    for w in range(WAVES):
        finish_a(3, w)
        over_tiles(w, make_stack([3]))

    for w in range(WAVES):
        for side in range(2):
            for h in range(2):
                for s in range(BLOCK + (side == h)):
                    z_copy(side, s, w, h).wait_send()
            for unit in range(4):
                x_first(side, unit, w).wait_send()
                x_second(side, unit, w).wait_send()
                y_first(side, unit, w).wait_send()
                y_second(side, unit, w).wait_send()
        for which in range(4):
            for unit in range(4):
                core_copy(which, unit, w).wait_send()


A_BLK = 32


def lag_kernel(stack, high, low, out):
    first = pl.program_id(0) * A_BLK
    rows = []
    for i in range(0, A_BLK, 2):
        start = pl.multiple_of((first + i) * TILES, 2 * TILES)
        flipped = stack[pl.ds(start, 2 * TILES), :].astype(jnp.bfloat16).T
        rows.append(jnp.concatenate([flipped[:64], flipped[64:]], axis=1))
    left = jnp.concatenate(rows, axis=0)
    lags = jnp.dot(left, high[...], preferred_element_type=jnp.float32)
    lags = lags + jnp.dot(left, low[...], preferred_element_type=jnp.float32)
    for i in range(0, A_BLK, 2):
        out[i, 0] = lags[32 * i : 32 * i + 64, :128]
        out[i + 1, 0] = lags[32 * i : 32 * i + 64, 128:]


def lag_tables():
    bins = np.arange(TILES)[:, None]
    lags = np.arange(128)[None, :]
    phases = (bins * lags % 128) * (2.0 * math.pi / 128)
    sines = -np.sin(phases)
    sines[0] = np.cos(math.pi * np.arange(128))
    table = np.zeros((2, 2, TILES, 2, 128))
    for i in range(2):
        table[0, i, :, i] = np.cos(phases)
        table[1, i, :, i] = sines
    table = table.reshape(4 * TILES, 256) / math.sqrt(128 * 128)
    high = table.astype(jnp.bfloat16)
    low = (table - high.astype(np.float64)).astype(jnp.bfloat16)
    return high, low


def body(spectra, kept_windows):
    dma = pltpu.SemaphoreType.DMA
    vmem = pl.BlockSpec(memory_space=pltpu.VMEM)
    stack = pl.pallas_call(
        gather_stack,
        out_shape=jax.ShapeDtypeStruct((128 * TILES, 128), jnp.float32),
        in_specs=[pl.BlockSpec(memory_space=pltpu.HBM)] * 2,
        out_specs=vmem,
        scratch_shapes=[
            pltpu.VMEM((16, 64, 16, 128), jnp.bfloat16),
            pltpu.VMEM((16, 2, 64, 16, 128), jnp.bfloat16),
            pltpu.VMEM((16, 64, 16, 128), jnp.bfloat16),
            pltpu.VMEM((TILES, 128, 512), jnp.bfloat16),
            pltpu.VMEM(spectra.shape, spectra.dtype),
            pltpu.VMEM((1, 128), jnp.int32),
            pltpu.VMEM((1024, 128), jnp.float32),
            pltpu.VMEM((5, 4, 8, 128), jnp.float32),
            pltpu.VMEM((1, 128), jnp.float32),
            dma((2, 5, 2, 2)), dma((2, 5, 2, 2)),
            dma((2, 4, 2)), dma((2, 4, 2)), dma((2, 4, 2)), dma((2, 4, 2)),
            dma((2, 4, 2)), dma((2, 4, 2)), dma((2, 4, 2)), dma((2, 4, 2)),
            dma((4, 4, 2)), dma((4, 4, 2)),
            dma((4, 2)), dma((2,)),
            dma((5, 4)), dma((5, 4)), dma((2,)),
        ],
        compiler_params=pltpu.CompilerParams(
            collective_id=0, has_side_effects=True, vmem_limit_bytes=40 << 20
        ),
        name="gather_stack",
    )(spectra, kept_windows.reshape(1, 128))
    high, low = lag_tables()
    return pl.pallas_call(
        lag_kernel,
        grid=(128 // A_BLK,),
        out_shape=jax.ShapeDtypeStruct((128, 1, 64, 128), jnp.float32),
        in_specs=[vmem, vmem, vmem],
        out_specs=pl.BlockSpec((A_BLK, 1, 64, 128), lambda i: (i, 0, 0, 0)),
        compiler_params=pltpu.CompilerParams(vmem_limit_bytes=40 << 20),
        name="lags",
    )(stack, jnp.asarray(high), jnp.asarray(low))


def solution(mesh):
    placed = (P(("row", "col"), None, None, None), P())
    return jax.shard_map(
        body, mesh=mesh, in_specs=placed, out_specs=P("row", "col", None, None), check_vma=False
    )
```

```python
import functools
import math

import jax
import jax.numpy as jnp
import numpy as np
from jax import lax
from jax.experimental import pallas as pl
from jax.experimental.pallas import tpu as pltpu
from jax.sharding import PartitionSpec as P

EPSILON = 1e-06
MESH = pl.DeviceIdType.MESH
WAVES = 2
CHUNK = 16
WAVE = 2 * CHUNK
BLOCK = 4
ORDER = [(1, 0)] + [(_w, _s) for _s in range(1, 5) for _w in range(WAVES)]
TILES = 64
STEP = 16


def gather_stack(spectra_hbm, kept_hbm, stack, zbuf, abuf, bbuf, rhs, spectra, kept, tmp, ebuf, factor,
                 zs, zr, xs, xr, xs2, xr2, ys, yr, ys2, yr2, cs, cr, la, lb, es, er, ls):
    row = lax.axis_index("row")
    col = lax.axis_index("col")
    x, zl = row // 4, row % 4
    zh, y, core = col // 8, (col // 2) % 4, col % 2
    z = zh * 4 + zl

    def at(dx=0, dy=0, dz=0, dzl=0, dzh=0, dc=0):
        new_z = (z + dz + 16) % 16
        new_zl = (new_z % 4 + dzl) % 4
        new_zh = (new_z // 4 + dzh) % 4
        return (
            (x + dx + 4) % 4 * 4 + new_zl,
            new_zh * 8 + (y + dy + 4) % 4 * 2 + (core + dc) % 2,
        )

    peers = [at(dz=1), at(dz=-1), at(dc=1)]
    for p in (1, 2, 3):
        peers += [at(dx=p), at(dy=p), at(dzl=p), at(dzh=p)]
    barrier = pltpu.get_barrier_semaphore()
    for peer in peers:
        pl.semaphore_signal(barrier, inc=1, device_id=peer, device_id_type=MESH)

    loads = [pltpu.make_async_copy(spectra_hbm, spectra, ls.at[0]), pltpu.make_async_copy(kept_hbm, kept, ls.at[1])]
    for load in loads:
        load.start()
    for load in loads:
        load.wait()

    channels = spectra.shape[0]
    to = lax.broadcasted_iota(jnp.int32, (TILES, TILES), 0)
    source = lax.broadcasted_iota(jnp.int32, (TILES, TILES), 1)
    mirror = ((to + source == TILES) | (to + source == 0)).astype(jnp.float32).astype(jnp.bfloat16)
    total = jnp.zeros((8, 128), jnp.float32)
    for part in range(2):
        for t in range(channels):
            plane = spectra[t, part].astype(jnp.float32)
            total = total + jnp.sum((plane * plane).reshape(16, 8, 128), axis=0)
            mirrored = jnp.dot(mirror, spectra[t, part, TILES:], preferred_element_type=jnp.float32)
            tmp[pl.ds(part * channels + t, TILES, stride=16), :] = plane[:TILES]
            tmp[pl.ds(8 + part * channels + t, TILES, stride=16), :] = mirrored
    zbuf[z] = tmp[...].reshape(TILES, 16, 128).astype(jnp.bfloat16)
    pl.semaphore_wait(barrier, len(peers))

    def remote(src, dst, send, recv, device):
        return pltpu.make_async_remote_copy(
            src_ref=src, dst_ref=dst, send_sem=send, recv_sem=recv, device_id=device, device_id_type=MESH
        )

    rounds = [("dx", x, 4), ("dy", y, 4), ("dzl", zl, 4), ("dzh", zh, 4), ("dc", core, 2)]

    def energy_copies(k):
        name, place, size = rounds[k]
        return [
            remote(ebuf.at[k, place], ebuf.at[k, place], es.at[k, p], er.at[k, p], at(**{name: p}))
            for p in range(1, size)
        ]

    def energy_start(k, value):
        ebuf[k, rounds[k][1]] = value
        for copy in energy_copies(k):
            copy.start()

    def energy_finish(k):
        for copy in energy_copies(k):
            copy.wait()
        return jnp.sum(ebuf[k, : rounds[k][2]], axis=0)

    def z_part(side, s, w, h):
        slot = (z - s + 16) % 16 if side == 0 else (z + s) % 16
        return zbuf.at[slot, pl.ds(w * WAVE + h * CHUNK, CHUNK)]

    def z_copy(side, s, w, h):
        part = z_part(side, s, w, h)
        hops = (1 if s < BLOCK else BLOCK) * (1 if side == 0 else -1)
        return remote(part, part, zs.at[side, s, w, h], zr.at[side, s, w, h], at(dz=hops))

    def z_arrived(side, s, w, h):
        part = z_part(side, s, w, h)
        sent = min(s - 1, BLOCK)
        remote(part, part, zs.at[side, sent, w, h], zr.at[side, sent, w, h], at(dz=1)).wait_recv()

    def wave(w):
        return pl.ds(w * WAVE, WAVE)

    def half(w, h):
        return pl.ds(w * WAVE + h * CHUNK, CHUNK)

    def x_first(side, unit, w):
        return remote(
            zbuf.at[zh * 4 + unit, wave(w)], bbuf.at[x * 4 + unit, wave(w)],
            xs.at[side, unit, w], xr.at[side, unit, w], at(dx=1 if side == 0 else -1),
        )

    def x_source(side, unit):
        return (x + (3 if side == 0 else 1)) % 4 * 4 + unit

    def x_arrived(side, unit, w):
        part = bbuf.at[x_source(side, unit), wave(w)]
        remote(part, part, xs.at[side, unit, w], xr.at[side, unit, w], at(dx=1)).wait_recv()

    def x_second(side, unit, w):
        part = bbuf.at[x_source(side, unit), half(w, side)]
        return remote(part, part, xs2.at[side, unit, w], xr2.at[side, unit, w], at(dx=1 if side == 0 else -1))

    def x_second_arrived(side, unit, w):
        part = bbuf.at[(x + 2) % 4 * 4 + unit, half(w, side)]
        remote(part, part, xs2.at[side, unit, w], xr2.at[side, unit, w], at(dx=1)).wait_recv()

    def z_high(unit):
        return (zh + (0, 3, 1, 2)[unit]) % 4

    def y_first(side, unit, w):
        return remote(
            zbuf.at[z_high(unit) * 4 + zl, wave(w)], abuf.at[z_high(unit) * 4 + y, core, wave(w)],
            ys.at[side, unit, w], yr.at[side, unit, w], at(dy=1 if side == 0 else -1),
        )

    def y_slot(unit, dy):
        return z_high(unit) * 4 + (y + dy + 4) % 4

    def y_arrived(side, unit, w):
        part = abuf.at[y_slot(unit, -1 if side == 0 else 1), core, wave(w)]
        remote(part, part, ys.at[side, unit, w], yr.at[side, unit, w], at(dy=1)).wait_recv()

    def y_second(side, unit, w):
        part = abuf.at[y_slot(unit, -1 if side == 0 else 1), core, half(w, side)]
        return remote(part, part, ys2.at[side, unit, w], yr2.at[side, unit, w], at(dy=1 if side == 0 else -1))

    def y_second_arrived(side, unit, w):
        part = abuf.at[y_slot(unit, 2), core, half(w, side)]
        remote(part, part, ys2.at[side, unit, w], yr2.at[side, unit, w], at(dy=1)).wait_recv()

    def core_copy(which, unit, w):
        slot = y_slot(unit, (0, -1, 1, 2)[which])
        src = zbuf.at[z_high(unit) * 4 + zl, wave(w)] if which == 0 else abuf.at[slot, core, wave(w)]
        return remote(src, abuf.at[slot, core, wave(w)], cs.at[which, unit, w], cr.at[which, unit, w], at(dc=1))

    def core_arrived(which, unit, w):
        slot = y_slot(unit, (0, -1, 1, 2)[which])
        part = abuf.at[slot, 1 - core, wave(w)]
        remote(part, part, cs.at[which, unit, w], cr.at[which, unit, w], at(dc=1)).wait_recv()

    def own_a(unit, w):
        return pltpu.make_async_copy(
            zbuf.at[z_high(unit) * 4 + zl, wave(w)], abuf.at[y_slot(unit, 0), core, wave(w)], la.at[unit, w]
        )

    def own_b(w):
        return pltpu.make_async_copy(
            zbuf.at[pl.ds(zh * 4, 4), wave(w)], bbuf.at[pl.ds(x * 4, 4), wave(w)], lb.at[w]
        )

    def y_send(unit, w):
        y_first(0, unit, w).start()
        y_first(1, unit, w).start()
        core_copy(0, unit, w).start()
        own_a(unit, w).start()

    def y_pass(unit, w):
        for side in range(2):
            y_arrived(side, unit, w)
            y_second(side, unit, w).start()
            core_copy(1 + side, unit, w).start()

    def y_end(unit, w):
        y_second_arrived(0, unit, w)
        y_second_arrived(1, unit, w)
        core_copy(3, unit, w).start()

    def x_send(unit, w):
        x_first(0, unit, w).start()
        x_first(1, unit, w).start()

    def x_pass(unit, w):
        for side in range(2):
            x_arrived(side, unit, w)
            x_second(side, unit, w).start()

    def in_block(s, act):
        if s == 0:
            act(zl)
        elif s < 4:
            pl.when(zl >= s)(lambda: act(zl - s))
            pl.when(zl + s < 4)(lambda: act(zl + s))

    def z_step(w, s):
        for h in range(2):
            for side in (h, 1 - h):
                if s > 0:
                    z_arrived(side, s, w, h)
                if s < BLOCK or side == h:
                    z_copy(side, s, w, h).start()
        if s == 0:
            y_send(0, w)
        if s == BLOCK:
            y_send(1, w)
            y_send(2, w)
        in_block(s, lambda unit: x_send(unit, w))
        if s == 3:
            own_b(w).start()
        if s >= 2:
            in_block(s - 2, lambda unit: x_pass(unit, w))
        if s == 2:
            y_pass(0, w)
        if s == 4:
            y_end(0, w)

    def z_last(w):
        for side in range(2):
            z_arrived(side, 2 * BLOCK, w, side)
        y_send(3, w)

    energy_start(0, total)
    z_step(0, 0)
    stage = 0
    for w, s in ORDER:
        z_step(w, s)
        if w == 0:
            energy_start(stage + 1, energy_finish(stage))
            stage += 1

    def finish_b(w):
        for unit in range(4):
            for side in range(2):
                x_second_arrived(side, unit, w)
        own_b(w).wait()

    def finish_a(unit, w):
        own_a(unit, w).wait()
        for which in range(4):
            core_arrived(which, unit, w)

    low_rows = lax.broadcasted_iota(jnp.int32, (1, 8, 128), 1) < 4

    def split_parts(both):
        even, odd = both[:, 0], both[:, 1]
        real = jnp.where(low_rows, even, pltpu.roll(odd, 4, 1))
        imag = jnp.where(low_rows, pltpu.roll(even, 4, 1), odd)
        return real.reshape(-1, 128), imag.reshape(-1, 128)

    def over_tiles(w, act):
        def step(i, carry):
            for k in range(STEP):
                act(w * WAVE + i * STEP + k)
            return carry

        lax.fori_loop(0, WAVE // STEP, step, 0)

    def make_rhs(tile):
        second = bbuf[:, tile].astype(jnp.float32).reshape(8, 2, 16, 128)
        real, imag = split_parts(second[:, :, :8])
        real_m, imag_m = split_parts(second[:, :, 8:])
        ends = tile == 0
        keep = jnp.where(ends, 0.0, 1.0)
        upper = jnp.concatenate([real, imag, real_m * keep, imag_m * keep], axis=1)
        lower = jnp.concatenate(
            [-imag * keep, real * keep, jnp.where(ends, real_m, imag_m), jnp.where(ends, imag_m, -real_m)], axis=1
        )
        rhs[tile] = jnp.concatenate([upper, lower], axis=0).astype(jnp.bfloat16)

    def make_stack(units):
        def act(tile):
            weight = factor[...]
            rows = []
            for unit in units:
                first = abuf[pl.ds(z_high(unit) * 4, 4), :, tile].astype(jnp.float32)
                parts = split_parts(first[:, :, :8]) + split_parts(first[:, :, 8:])
                rows.append(jnp.concatenate([part * weight for part in parts], axis=1).astype(jnp.bfloat16))
            sums = lax.dot_general(
                jnp.concatenate(rows, axis=0), rhs[tile], (((1,), (1,)), ((), ())), preferred_element_type=jnp.float32
            )
            for i, unit in enumerate(units):
                stack[pl.ds(z_high(unit) * (32 * TILES) + tile, 32, stride=TILES), :] = sums[32 * i : 32 * i + 32]

        return act

    for w in range(WAVES):
        in_block(3, lambda unit: x_pass(unit, w))
    for w in range(WAVES):
        y_pass(1, w)
        y_pass(2, w)
    value = energy_finish(4)
    members = channels * lax.axis_size("row") * lax.axis_size("col")
    energy = jnp.sum(value, axis=0, keepdims=True) / (members * 2 * 128) + EPSILON
    factor[...] = kept[...].astype(jnp.float32) / energy
    for w in range(WAVES):
        finish_b(w)
        over_tiles(w, make_rhs)
        y_end(1, w)
        y_end(2, w)
        z_last(w)
    y_pass(3, 0)
    for w in range(WAVES):
        finish_a(0, w)
        finish_a(1, w)
        finish_a(2, w)
        over_tiles(w, make_stack([0, 1, 2]))
        if w == 0:
            y_pass(3, 1)
            y_end(3, 0)
    y_end(3, 1)
    for w in range(WAVES):
        finish_a(3, w)
        over_tiles(w, make_stack([3]))

    for w in range(WAVES):
        for side in range(2):
            for h in range(2):
                for s in range(BLOCK + (side == h)):
                    z_copy(side, s, w, h).wait_send()
            for unit in range(4):
                x_first(side, unit, w).wait_send()
                x_second(side, unit, w).wait_send()
                y_first(side, unit, w).wait_send()
                y_second(side, unit, w).wait_send()
        for which in range(4):
            for unit in range(4):
                core_copy(which, unit, w).wait_send()


A_BLK = 64


def lag_kernel(stack, high, low, out):
    first = pl.program_id(0) * A_BLK
    rows = []
    for i in range(0, A_BLK, 2):
        start = pl.multiple_of((first + i) * TILES, 2 * TILES)
        flipped = stack[pl.ds(start, 2 * TILES), :].astype(jnp.bfloat16).T
        rows.append(jnp.concatenate([flipped[:64], flipped[64:]], axis=1))
    left = jnp.concatenate(rows, axis=0)
    lags = jnp.dot(left, high[...], preferred_element_type=jnp.float32)
    lags = lags + jnp.dot(left, low[...], preferred_element_type=jnp.float32)
    for i in range(0, A_BLK, 2):
        out[i, 0] = lags[32 * i : 32 * i + 64, :128]
        out[i + 1, 0] = lags[32 * i : 32 * i + 64, 128:]


def lag_tables():
    bins = np.arange(TILES)[:, None]
    lags = np.arange(128)[None, :]
    phases = (bins * lags % 128) * (2.0 * math.pi / 128)
    sines = -np.sin(phases)
    sines[0] = np.cos(math.pi * np.arange(128))
    table = np.zeros((2, 2, TILES, 2, 128))
    for i in range(2):
        table[0, i, :, i] = np.cos(phases)
        table[1, i, :, i] = sines
    table = table.reshape(4 * TILES, 256) / math.sqrt(128 * 128)
    high = table.astype(jnp.bfloat16)
    low = (table - high.astype(np.float64)).astype(jnp.bfloat16)
    return high, low


def body(spectra, kept_windows):
    dma = pltpu.SemaphoreType.DMA
    vmem = pl.BlockSpec(memory_space=pltpu.VMEM)
    stack = pl.pallas_call(
        gather_stack,
        out_shape=jax.ShapeDtypeStruct((128 * TILES, 128), jnp.float32),
        in_specs=[pl.BlockSpec(memory_space=pltpu.HBM)] * 2,
        out_specs=vmem,
        scratch_shapes=[
            pltpu.VMEM((16, 64, 16, 128), jnp.bfloat16),
            pltpu.VMEM((16, 2, 64, 16, 128), jnp.bfloat16),
            pltpu.VMEM((16, 64, 16, 128), jnp.bfloat16),
            pltpu.VMEM((TILES, 128, 512), jnp.bfloat16),
            pltpu.VMEM(spectra.shape, spectra.dtype),
            pltpu.VMEM((1, 128), jnp.int32),
            pltpu.VMEM((1024, 128), jnp.float32),
            pltpu.VMEM((5, 4, 8, 128), jnp.float32),
            pltpu.VMEM((1, 128), jnp.float32),
            dma((2, 5, 2, 2)), dma((2, 5, 2, 2)),
            dma((2, 4, 2)), dma((2, 4, 2)), dma((2, 4, 2)), dma((2, 4, 2)),
            dma((2, 4, 2)), dma((2, 4, 2)), dma((2, 4, 2)), dma((2, 4, 2)),
            dma((4, 4, 2)), dma((4, 4, 2)),
            dma((4, 2)), dma((2,)),
            dma((5, 4)), dma((5, 4)), dma((2,)),
        ],
        compiler_params=pltpu.CompilerParams(
            collective_id=0, has_side_effects=True, vmem_limit_bytes=40 << 20
        ),
        name="gather_stack",
    )(spectra, kept_windows.reshape(1, 128))
    high, low = lag_tables()
    return pl.pallas_call(
        lag_kernel,
        grid=(128 // A_BLK,),
        out_shape=jax.ShapeDtypeStruct((128, 1, 64, 128), jnp.float32),
        in_specs=[vmem, vmem, vmem],
        out_specs=pl.BlockSpec((A_BLK, 1, 64, 128), lambda i: (i, 0, 0, 0)),
        compiler_params=pltpu.CompilerParams(vmem_limit_bytes=40 << 20),
        name="lags",
    )(stack, jnp.asarray(high), jnp.asarray(low))


def solution(mesh):
    placed = (P(("row", "col"), None, None, None), P())
    return jax.shard_map(
        body, mesh=mesh, in_specs=placed, out_specs=P("row", "col", None, None), check_vma=False
    )
```
